32 devices in a mesh: groups: 2 (over y), leaf: 4 (over z), sub: 2 (over x), vec: 2 (over core).
Axes of the slice: x: 2, y: 2, z: 4, core: 2. Of those that a mesh axis runs over, the one named last changes fastest.
Arguments:
- vectors: bfloat16 [32, 131072], P('vec', ('groups', 'leaf', 'sub')), parts along dimension 1, may hold values from -6 to 6
- points: float32 [3, 131072], P(None, ('groups', 'leaf', 'sub')), parts along dimension 1, as said below
- leaf_basis: bfloat16 [32, 131072], P(None, ('groups', 'leaf', 'sub')), parts along dimension 1, may hold values from -0.75 to 0.75
- transfer: float32 [8, 32, 32], replicated, may hold values from -1 to 1
- proxy_points: float32 [3, 32], replicated, may hold values from -0.5 to 0.5
- near_list: int32 [2048, 27], P(('groups', 'leaf', 'sub')), parts along dimension 0, may hold values from -1 to 1023, as said below
- far_leaf: int32 [2048, 64], P(('groups', 'leaf', 'sub')), parts along dimension 0, may hold values from -1 to 1023, as said below
- far_mid: int32 [256, 12], P(('groups', 'leaf', 'sub')), parts along dimension 0, may hold values from -1 to 127, as said below
- far_root: int32 [32, 3], P(('groups', 'leaf', 'sub')), parts along dimension 0, may hold values from -1 to 15, as said below
- far_top: int32 [8, 3], P('groups'), parts along dimension 0, may hold values from -1 to 3, as said below
Outputs:
- field: float32 [32, 131072], P('vec', ('groups', 'leaf', 'sub')), parts along dimension 1
The draws below stay inside these ranges and needn't reach their ends.
There are 2 independent parts, one for each index of `groups`. The reference program is written for one: setup_inputs(seed, part) draws one part's arguments, and reference() takes and returns one part's arrays. A program takes and returns all parts, laid end to end along the dimension named above; an argument that names none is the same for every part. Nothing has to cross between parts.
Inputs may be any that keep to these rules, and one draw needn't show every extreme that they name: The points of leaf i lie in the unit cube whose corner is leaf i's cell in Morton order. `near_list`: entry 0 of row i is i; every other entry is -1 or a leaf whose cell touches leaf i's cell (by a face, an edge or a corner) and whose index differs from i by 1 to 127, each named once in a row; -1 entries stand after all others. `far_leaf`: each entry is -1 or a leaf whose index differs from the row's by 1 to 127; -1 entries stand after all others. `far_mid`: each entry is -1 or a mid node whose index differs from the row's by 1 to 15; -1 entries stand after all others. `far_root`: each entry is -1 or another root below the same top node, each named once in a row; -1 entries stand after all others. `far_top`: each entry is -1 or another top node, each named once in a row; -1 entries stand after all others.
All inputs are finite; a program needn't handle non-finite values.
Results may differ from the reference program's by a relative error of at most 0.0027.
The reference program's roundings to bfloat16 on the way (of `coarse` and `weights`) count: a program that leaves them out, or rounds other values in their place, can miss the bound.
Values may be sent and summed in bfloat16 or wider, within the bound.
No kernel may reach another device: no remote copies, remote signals or barrier semaphores. Data moves between devices by JAX's collectives and lax.ppermute only.
A program may use at most 64 MiB of HBM per device.

```python
import math
import jax
import jax.numpy as jnp
import numpy as np
from jax import lax

PTS = 64
RANK = 32
V = 32
NEAR = 27
F0 = 64
F1 = 12
MID_DEV = 16
LEAF_DEV = 128
CH = 4
F2 = 3
F3 = 3
ROOTS = 16
MIDS = 128
LEAVES = 1024
NPTS = 65536
TOPS = 4


def morton_cells(leaf_ids):
    cells = []
    for axis_number in range(3):
        position = jnp.zeros_like(leaf_ids)
        for bit_number in range(8):
            picked = jnp.bitwise_and(jnp.right_shift(leaf_ids, 3 * bit_number + axis_number), 1)
            position = position + jnp.left_shift(picked, bit_number)
        cells.append(position)
    return cells


def morton_code(cells):
    code = jnp.zeros_like(cells[0])
    for axis_number in range(3):
        for bit_number in range(8):
            picked = jnp.bitwise_and(jnp.right_shift(cells[axis_number], bit_number), 1)
            code = code + jnp.left_shift(picked, 3 * bit_number + axis_number)
    return code


def neighbour_steps():
    steps = [(0, 0, 0)]
    for first in (-1, 0, 1):
        for second in (-1, 0, 1):
            for third in (-1, 0, 1):
                if first != 0 or second != 0 or third != 0:
                    steps.append((first, second, third))
    return np.array(steps, dtype=np.int32)


def offset_partners(key, rows, slot_count, span, self_first):
    keys = jax.random.split(key, 3)
    row_ids = jnp.arange(rows, dtype=jnp.int32)[:, None]
    slot_ids = jnp.arange(slot_count, dtype=jnp.int32)[None, :]
    distance = jax.random.randint(keys[0], (rows, slot_count), 1, span)
    direction = jax.random.randint(keys[1], (rows, slot_count), 0, 2) * 2 - 1
    candidate = row_ids + direction * distance
    outside = (candidate < 0) | (candidate >= rows)
    candidate = jnp.where(outside, row_ids - direction * distance, candidate)
    filled = jax.random.randint(keys[2], (rows, 1), (slot_count + 1) // 2, slot_count + 1)
    filled = jnp.where(row_ids % span == 0, slot_count, filled)
    if self_first:
        candidate = jnp.where(slot_ids == 0, row_ids, candidate)
    return jnp.where(slot_ids < filled, candidate, -1).astype(jnp.int32)


def sibling_partners(key, rows, group, slot_count):
    keys = jax.random.split(key, 2)
    shuffled = jax.vmap(lambda sub_key: jax.random.permutation(sub_key, group - 1))(jax.random.split(keys[0], rows))
    shuffled = shuffled[:, :slot_count].astype(jnp.int32)
    row_ids = jnp.arange(rows, dtype=jnp.int32)[:, None]
    slot_ids = jnp.arange(slot_count, dtype=jnp.int32)[None, :]
    first_row = row_ids - row_ids % group
    candidate = first_row + (row_ids % group + 1 + shuffled) % group
    filled = jax.random.randint(keys[1], (rows, 1), slot_count // 2, slot_count + 1)
    filled = jnp.where(row_ids % group == 0, slot_count, filled)
    return jnp.where(slot_ids < filled, candidate, -1).astype(jnp.int32)


def draw_points(key, part):
    key = jax.random.fold_in(key, 3)
    leaf_ids = jnp.arange(NPTS, dtype=jnp.int32) // PTS
    cells = morton_cells(leaf_ids)
    corner = jnp.stack([cell.astype(jnp.float32) for cell in cells], axis=0)
    jitter = jax.random.uniform(key, (3, NPTS), jnp.float32)
    return (corner + jitter).astype(jnp.float32)


def draw_near_list(key, part):
    key = jax.random.fold_in(key, 5)
    keys = jax.random.split(key, 2)
    steps = jnp.asarray(neighbour_steps())
    step_count = steps.shape[0]
    row_ids = jnp.arange(LEAVES, dtype=jnp.int32)
    own_cells = morton_cells(row_ids)
    inside = jnp.ones((LEAVES, step_count), dtype=bool)
    moved = []
    for axis_number in range(3):
        coordinate = own_cells[axis_number][:, None] + steps[:, axis_number][None, :]
        inside = inside & (coordinate >= 0) & (coordinate < 256)
        moved.append(jnp.clip(coordinate, 0, 255).astype(jnp.int32))
    candidate = morton_code(moved).astype(jnp.int32)
    gap = jnp.abs(candidate - row_ids[:, None])
    slot_ids = jnp.arange(step_count, dtype=jnp.int32)[None, :]
    kept = jax.random.randint(keys[0], (LEAVES, step_count), 0, 8) > 0
    valid = inside & (candidate < LEAVES) & (gap < LEAF_DEV) & (kept | (slot_ids == 0))
    score = jax.random.randint(keys[1], (LEAVES, step_count), 0, 1024) * 64 + slot_ids
    score = jnp.where(valid, score, 1048576 + slot_ids)
    score = jnp.where(slot_ids == 0, -1, score).astype(jnp.int32)
    order = jnp.argsort(score, axis=1, stable=True)
    listed = jnp.take_along_axis(jnp.where(valid, candidate, -1), order, axis=1)
    return listed[:, :NEAR].astype(jnp.int32)


def draw_far_leaf(key, part):
    key = jax.random.fold_in(key, 7)
    return offset_partners(key, LEAVES, F0, LEAF_DEV, False)


def draw_far_mid(key, part):
    key = jax.random.fold_in(key, 9)
    return offset_partners(key, MIDS, F1, MID_DEV, False)


def draw_far_root(key, part):
    key = jax.random.fold_in(key, 11)
    return sibling_partners(key, ROOTS, CH, F2)


def draw_far_top(key, part):
    key = jax.random.fold_in(key, 13)
    return sibling_partners(key, TOPS, TOPS, F3)


def levels(stream_key, shape, pieces, smallest, high):
    def one(dim, parts):
        draws = jax.random.uniform(jax.random.fold_in(jax.random.fold_in(stream_key, 6), dim), (parts,), jnp.float32, smallest / len(pieces), high / len(pieces))
        return jnp.repeat(jnp.exp(draws), shape[dim] // parts).reshape((-1,) + (1,) * (len(shape) - dim - 1))

    gain = one(*pieces[0])
    for cut in pieces[1:]:
        gain = gain * one(*cut)
    return gain


def gaussian(key, dims, scale, bound, cuts=(), kind=jnp.bfloat16):
    values = jax.random.normal(key, dims, jnp.float32) * scale
    if len(cuts) > 0:
        values = levels(key, dims, cuts, -0.22, 0.18) * values
    return jnp.clip(values, min=-bound, max=bound).astype(kind)


def setup_inputs(seed: int = 0, part: int = 0) -> dict:
    streams_of = jax.random.split(jax.random.key(seed), 11)
    part_splits = jax.random.split(jax.random.fold_in(streams_of[10], part), 11)
    vectors = gaussian(part_splits[0], (V, NPTS), 1.0, 6.0, ((0, 2), (1, 8)))
    points = draw_points(jax.random.fold_in(jax.random.fold_in(streams_of[10], part), 71), part)
    leaf_basis = gaussian(part_splits[2], (RANK, NPTS), PTS ** -0.5, 0.75, ((1, 8),))
    transfer = gaussian(streams_of[3], (8, RANK, RANK), RANK ** -0.5, 1.0, (), jnp.float32)
    proxy_points = jnp.clip(jax.random.uniform(streams_of[4], (3, RANK), jnp.float32, -0.5, 0.5), -0.5, 0.5)
    near_list = draw_near_list(jax.random.fold_in(jax.random.fold_in(streams_of[10], part), 71), part)
    far_leaf = draw_far_leaf(jax.random.fold_in(jax.random.fold_in(streams_of[10], part), 71), part)
    far_mid = draw_far_mid(jax.random.fold_in(jax.random.fold_in(streams_of[10], part), 71), part)
    far_root = draw_far_root(jax.random.fold_in(jax.random.fold_in(streams_of[10], part), 71), part)
    far_top = draw_far_top(jax.random.fold_in(jax.random.fold_in(streams_of[10], part), 71), part)
    return {"vectors": vectors, "points": points, "leaf_basis": leaf_basis, "transfer": transfer, "proxy_points": proxy_points, "near_list": near_list, "far_leaf": far_leaf, "far_mid": far_mid, "far_root": far_root, "far_top": far_top}


SOFTENING = 0.25
INV_FOUR_PI = 0.25 / math.pi

def pair_kernel(squared):
    return INV_FOUR_PI / jnp.sqrt(squared + SOFTENING * SOFTENING)

def near_field(window_values, window_points, target_points, partner_lists, shift_rows):
    channels = window_values.shape[0]
    targets = partner_lists.shape[0]
    slot_count = partner_lists.shape[1]
    per_leaf = target_points.shape[1] // targets
    source_values = window_values.reshape(channels, -1, per_leaf)
    source_points = window_points.astype(jnp.float32).reshape(3, -1, per_leaf)
    block_size = min(targets, max(16, targets // 16))
    turn_count = targets // block_size
    target_blocks = target_points.astype(jnp.float32).reshape(3, turn_count, block_size, per_leaf).transpose(1, 0, 2, 3)
    list_blocks = partner_lists.reshape(turn_count, block_size, slot_count)

    def one_block(operands):
        target_block, list_block = operands
        present = list_block >= 0
        local_rows = jnp.where(present, list_block - shift_rows, 0)
        gathered = source_points[:, local_rows].reshape(3, block_size, 1, slot_count * per_leaf)
        squared = jnp.zeros((block_size, per_leaf, slot_count * per_leaf), jnp.float32)
        for component in range(3):
            offset = target_block[component][:, :, None] - gathered[component]
            squared = squared + offset * offset
        weight_mask = jnp.repeat(present.astype(jnp.float32), per_leaf, axis=1)[:, None, :]
        weights = (pair_kernel(squared) * weight_mask).astype(jnp.bfloat16)
        values = source_values[:, local_rows].reshape(channels, block_size, slot_count * per_leaf)
        return jnp.einsum('bpm,wbm->wbp', weights.astype(jnp.float32), values.astype(jnp.float32), precision=lax.Precision.HIGHEST)
    results = lax.map(one_block, (target_blocks, list_blocks))
    return results.transpose(1, 0, 2, 3).reshape(channels, targets * per_leaf)

def couple(coefficients, centres, own_centres, partner_lists, shift_rows, radius, proxy_points):
    node_count, slot_count = partner_lists.shape
    rank_width = proxy_points.shape[1]
    block_size = min(node_count, 16)
    turn_count = node_count // block_size
    own_blocks = own_centres.reshape(3, turn_count, block_size).transpose(1, 0, 2)
    list_blocks = partner_lists.reshape(turn_count, block_size, slot_count)

    def one_block(operands):
        own_block, list_block = operands
        present = list_block >= 0
        local_rows = jnp.where(present, list_block - shift_rows, 0)
        far_centres = centres[:, local_rows]
        squared = jnp.zeros((block_size, slot_count, rank_width, rank_width), jnp.float32)
        for component in range(3):
            target = own_block[component][:, None, None] + radius * proxy_points[component][None, None, :]
            source = far_centres[component][:, :, None] + radius * proxy_points[component][None, None, :]
            offset = target[:, :, :, None] - source[:, :, None, :]
            squared = squared + offset * offset
        weights = pair_kernel(squared) * present.astype(jnp.float32)[:, :, None, None]
        return jnp.einsum('bfrs,bfsv->brv', weights, coefficients[local_rows], precision=lax.Precision.HIGHEST)
    results = lax.map(one_block, (own_blocks, list_blocks))
    return results.reshape(node_count, rank_width, -1)

def upward(children, matrices):
    branch = matrices.shape[0]
    grouped = children.reshape(-1, branch, children.shape[1], children.shape[2])
    return jnp.einsum('csr,ncsv->nrv', matrices, grouped, precision=lax.Precision.HIGHEST)

def downward(parents, matrices):
    spread = jnp.einsum('crs,nsv->ncrv', matrices, parents, precision=lax.Precision.HIGHEST)
    return spread.reshape(-1, parents.shape[1], parents.shape[2])

def reference(vectors, points, leaf_basis, transfer, proxy_points, near_list, far_leaf, far_mid, far_root, far_top):
    leaves = near_list.shape[0]
    per_leaf = points.shape[1] // leaves
    basis_blocks = leaf_basis.reshape(RANK, leaves, per_leaf).astype(jnp.float32)
    leaf_coef = jnp.einsum('rlp,vlp->lrv', basis_blocks, vectors.reshape(V, leaves, per_leaf).astype(jnp.float32), precision=lax.Precision.HIGHEST)
    mid_coef = upward(leaf_coef, transfer)
    root_coef = upward(mid_coef, transfer)
    top_table = transfer[np.arange(CH) % 8]
    top_coef = upward(root_coef, top_table)
    leaf_centre = lax.optimization_barrier(jnp.mean(points.astype(jnp.float32).reshape(3, leaves, per_leaf), axis=2))
    mid_centre = lax.optimization_barrier(jnp.mean(leaf_centre.reshape(3, -1, 8), axis=2))
    root_centre = lax.optimization_barrier(jnp.mean(mid_centre.reshape(3, -1, 8), axis=2))
    top_centre = lax.optimization_barrier(jnp.mean(root_centre.reshape(3, -1, CH), axis=2))
    top_out = couple(top_coef, top_centre, top_centre, far_top, 0, 8.0, proxy_points)
    root_out = couple(root_coef, root_centre, root_centre, far_root, 0, 4.0, proxy_points) + downward(top_out, top_table)
    mid_out = couple(mid_coef, mid_centre, mid_centre, far_mid, 0, 2.0, proxy_points) + downward(root_out, transfer)
    leaf_out = couple(leaf_coef, leaf_centre, leaf_centre, far_leaf, 0, 1.0, proxy_points) + downward(mid_out, transfer)
    coarse = leaf_out.astype(jnp.bfloat16)
    far_part = jnp.einsum('rlp,lrv->vlp', basis_blocks, coarse.astype(jnp.float32), precision=lax.Precision.HIGHEST).reshape(V, -1)
    near_part = near_field(vectors, points, points, near_list, 0)
    return near_part + far_part
```

```python
import functools
import math

import jax
import jax.numpy as jnp
import numpy as np
from jax import lax
from jax.experimental import pallas as pl
from jax.experimental.pallas import tpu as pltpu
from jax.sharding import PartitionSpec as P

F32 = jnp.float32
BF16 = jnp.bfloat16
SCALE = 4.0 * math.pi
SOFT = (SCALE * 0.25) ** 2
HI = lax.Precision.HIGHEST
NN = (((1,), (0,)), ((), ()))
NT = (((1,), (1,)), ((), ()))
PAIRS = 16
ROW_X, ROW_P, ROW_C, ROW_MH, ROW_ML, ROW_K, ROWS = 0, 256, 512, 1024, 1088, 1152, 1168
UNEAR = 8
UFAR = 8


def dot(a, b, dims=NN, precision=None):
    return lax.dot_general(a, b, dims, precision=precision, preferred_element_type=F32)


def iota(shape, dim):
    return lax.broadcasted_iota(jnp.int32, shape, dim)


def rounded(x):
    return x.astype(BF16).astype(F32)


def pieces(x):
    high = rounded(x)
    rest = x - high
    mid = rounded(rest)
    return high, mid, rounded(rest - mid)


def rows8(x3):
    zero = jnp.zeros((1, x3.shape[1]), F32)
    return jnp.concatenate([x3, zero, x3, zero], axis=0)


def pack16(x8):
    high, mid, low = pieces(x8)
    first = jnp.where(iota(x8.shape, 0) < 4, high, mid)
    return jnp.concatenate([first, low], axis=0).astype(BF16)


def unpack16(x16):
    x16 = x16.astype(F32)
    first, low = x16[:8], x16[8:]
    return first + pltpu.roll(first, 4, 0) + low


def with_norm(u8, extra):
    square = u8 * u8
    norm = pltpu.roll(square, 1, 0) + pltpu.roll(square, 2, 0) + pltpu.roll(square, 3, 0)
    return jnp.where(iota(u8.shape, 0) % 4 == 3, norm + extra, u8)


def source_rows(u8):
    high, mid, low = pieces(with_norm(u8, 0.0))
    row = iota(u8.shape, 0)
    a = jnp.where(row < 4, high, mid)
    b = jnp.where(row % 4 == 3, 1.0, a)
    c = jnp.where(row < 4, low, jnp.where(row == 7, 1.0, high))
    return jnp.concatenate([a, b, c, jnp.zeros_like(a)], axis=0)


def target_rows(u8):
    high, mid, low = pieces(with_norm(u8, SOFT))
    row = iota(u8.shape, 0)
    a = jnp.where(row % 4 == 3, 1.0, -2.0 * high)
    b = jnp.where(row == 3, high, jnp.where(row == 7, mid, -2.0 * mid))
    c = jnp.where(
        row < 3,
        -2.0 * high,
        jnp.where(row == 3, 1.0, jnp.where(row == 7, low, -2.0 * low)),
    )
    return jnp.concatenate([a, b, c, jnp.zeros_like(a)], axis=0)


def eye(n):
    return (iota((n, n), 0) == iota((n, n), 1)).astype(BF16)


def turned(rows32, identity):
    return dot(identity, rows32.astype(BF16), NT).astype(BF16)


def origin8(base):
    out = []
    for axis in range(3):
        cell = jnp.int32(0)
        for bit in range(8):
            cell = cell + ((base >> (3 * bit + axis)) & 1) * (1 << bit)
        out.append(cell.astype(F32) + (4.0 if axis == 0 else 2.0))
    row = iota((8, 128), 0) % 4
    return jnp.where(
        row == 0, out[0], jnp.where(row == 1, out[1], jnp.where(row == 2, out[2], 0.0))
    )


def four_tiled(nat, group):
    turns = [nat] + [pltpu.roll(nat, 32 * k, 1) for k in (1, 2, 3)]
    out = []
    for h in range(4):
        pick = [turns[(q - h) % 4] for q in range(4)]
        out.append(
            jnp.where(
                group < 2,
                jnp.where(group == 0, pick[0], pick[1]),
                jnp.where(group == 2, pick[2], pick[3]),
            )
        )
    return out


def expand_centres(c8, tiles):
    spread = (iota((128, 128), 0) == iota((128, 128), 1) // 32).astype(F32)
    stack = [c8 if t == 0 else pltpu.roll(c8, 128 - 4 * t, 1) for t in range(tiles)]
    return dot(jnp.concatenate(stack, axis=0), spread, precision=HI)


def diagonal_basis(basis):
    leaf = iota((32, 256), 1) // 64
    zero = jnp.zeros_like(basis)
    return jnp.concatenate([jnp.where(leaf == h, basis, zero) for h in range(4)], axis=0)


def items_of(counts, slots):
    groups = jnp.floor((counts + (slots - 1)) * (1.0 / slots))
    wide = jnp.broadcast_to(groups, (128, 128))
    lower = (iota((128, 128), 1) <= iota((128, 128), 0)).astype(BF16)
    ends = dot(lower, wide.astype(BF16))
    out = []
    for t in range(8):
        k = (iota((128, 128), 1) + 128 * t).astype(F32)
        passed = jnp.where(ends <= k, 1.0, 0.0)
        leaf = jnp.sum(passed, axis=0, keepdims=True)
        start = jnp.sum(passed * wide, axis=0, keepdims=True)
        group = jnp.where(leaf >= 128.0, 0.0, k[:1] - start)
        out.append(leaf * 16.0 + group)
    out = jnp.concatenate(out + [ends[127:128]], axis=0)
    return jnp.concatenate([out, jnp.zeros((7, 128), F32)], axis=0).astype(jnp.int32)


def local_kernel(
    dev_ref,
    pair_ref,
    vec_ref,
    pts_ref,
    basis_ref,
    transfer_ref,
    near_ref,
    far_ref,
    ahead_ref,
    back_ref,
    root_ref,
    coef_ref,
    mid_ref,
    centre_ref,
    near_items_ref,
    far_items_ref,
    near_out_ref,
    far_out_ref,
    p8_ref,
):
    dev = dev_ref[0]
    base = dev * 128
    lane = iota((8, 128), 1)
    group = iota((16, 128), 1) // 32
    near = near_ref[...]
    far = far_ref[...]
    near_items_ref[...] = items_of(
        jnp.sum(jnp.where(near >= 0, 1.0, 0.0), axis=1, keepdims=True), 4
    )
    far_items_ref[...] = items_of(
        jnp.sum(jnp.where(far >= 0, 1.0, 0.0), axis=1, keepdims=True), 8
    )
    near_out_ref[...] = jnp.full(near_out_ref.shape, 384, jnp.int32)
    near_out_ref[0:128, 0 : near.shape[1]] = jnp.where(near >= 0, near - base + 128, 384)
    far_out_ref[...] = jnp.full(far_out_ref.shape, 384, jnp.int32)
    far_out_ref[0:128, 0 : far.shape[1]] = jnp.where(far >= 0, far - base + 128, 384)
    mids = []
    four_e = jnp.concatenate([transfer_ref[...]] * 4, axis=1)
    rows = []
    for t in range(32):
        cols = slice(256 * t, 256 * t + 256)
        nat = dot(vec_ref[:, cols], diagonal_basis(basis_ref[:, cols]), NT)
        coef_ref[16 * t : 16 * t + 16, :] = nat.astype(BF16)
        rows.append(nat)
    stack = jnp.concatenate(
        [jnp.concatenate([rows[2 * m], rows[2 * m + 1]], axis=1) for m in range(16)], axis=0
    )
    mids = dot(stack, four_e, precision=HI)
    mid_nat = []
    for t in range(4):
        part = [mids[16 * (4 * t + h) : 16 * (4 * t + h) + 16] for h in range(4)]
        mid_nat.append(
            jnp.where(
                group < 2,
                jnp.where(group == 0, part[0], part[1]),
                jnp.where(group == 2, part[2], part[3]),
            )
        )
    roots = dot(
        jnp.concatenate(
            [jnp.concatenate([mid_nat[0], mid_nat[1]], axis=1),
             jnp.concatenate([mid_nat[2], mid_nat[3]], axis=1)], axis=0),
        four_e,
        precision=HI,
    )
    root_ref[0:32, :] = roots
    for t in range(4):
        high = mid_nat[t].astype(BF16)
        mid_ref[16 * t : 16 * t + 16, :] = high
        mid_ref[64 + 16 * t : 64 + 16 * t + 16, :] = (mid_nat[t] - high.astype(F32)).astype(BF16)
    c8 = jnp.zeros((8, 128), F32)
    for t in range(64):
        p8 = rows8(pts_ref[:, 128 * t : 128 * t + 128])
        p8_ref[:, 128 * t : 128 * t + 128] = p8
        total = p8
        for shift in (32, 16, 8, 4, 2, 1):
            total = total + pltpu.roll(total, 128 - shift, 1)
        even = pltpu.roll(total, 2 * t, 1) if t else total
        odd = pltpu.roll(total, (2 * t + 1 + 64) % 128, 1)
        c8 = jnp.where(lane == 2 * t, even, jnp.where(lane == 2 * t + 1, odd, c8))
    c8 = c8 * (1.0 / 64.0)
    centre_ref[...] = pack16(c8)
    for b in range(2):
        mean = jnp.sum(jnp.where(lane // 64 == b, c8, 0.0), axis=1, keepdims=True) * (1.0 / 64.0)
        root_ref[32 + 8 * b : 40 + 8 * b, :] = jnp.broadcast_to(mean, (8, 128))
    for way, msg_ref in enumerate((ahead_ref, back_ref)):
        for k in range(PAIRS):
            at = pl.multiple_of(pair_ref[dev, way * PAIRS + k] * 128, 128)
            msg_ref[ROW_X + 16 * k : ROW_X + 16 * k + 16, :] = vec_ref[:, pl.ds(at, 128)]
            msg_ref[ROW_P + 16 * k : ROW_P + 16 * k + 16, :] = pack16(p8_ref[:, pl.ds(at, 128)])
        msg_ref[ROW_C : ROW_C + 512, :] = coef_ref[...]
        msg_ref[ROW_MH : ROW_MH + 128, :] = mid_ref[...]
        msg_ref[ROW_K : ROW_K + 16, :] = centre_ref[...]


def near_kernel(
    dev_ref,
    item_ref,
    list_ref,
    map_ref,
    vec_ref,
    pts_ref,
    prev_ref,
    next_ref,
    out_ref,
    table_ref,
    target_ref,
    sum_ref,
):
    dev = dev_ref[0]
    origin = origin8(dev * 128)
    identity = eye(128)
    low = iota((48, 128), 1) < 64

    def put(row, x, rows):
        both = jnp.concatenate([x.astype(F32), rows], axis=0)
        other = pltpu.roll(both, 64, 1)
        table_ref[row] = jnp.where(low, both, other).astype(BF16)
        table_ref[row + 1] = jnp.where(low, other, both).astype(BF16)

    for t in range(64):
        cols = slice(128 * t, 128 * t + 128)
        u8 = (rows8(pts_ref[:, cols]) - origin) * SCALE
        u8 = jnp.where(iota((8, 128), 0) % 4 == 3, 0.0, u8)
        put(2 * t, vec_ref[:, cols], source_rows(u8))
        turn = turned(target_rows(u8), identity)
        target_ref[2 * t] = turn[:64]
        target_ref[2 * t + 1] = turn[64:]
    for way, msg_ref in enumerate((prev_ref, next_ref)):
        for k in range(PAIRS):
            p8 = unpack16(msg_ref[ROW_P + 16 * k : ROW_P + 16 * k + 16, :])
            u8 = (p8 - origin) * SCALE
            put(
                128 + 2 * (PAIRS * way + k),
                msg_ref[ROW_X + 16 * k : ROW_X + 16 * k + 16, :],
                source_rows(u8),
            )
    table_ref[192] = jnp.where(iota((48, 128), 0) < 16, 0.0, table_ref[0].astype(F32)).astype(BF16)
    target_ref[128] = target_ref[0]
    sum_ref[...] = jnp.zeros_like(sum_ref)

    def step(it, carry):
        for u in range(UNEAR):
            k = it * UNEAR + u
            packed = item_ref[k >> 7, k & 127]
            leaf = packed >> 4
            col = (packed & 15) * 4
            part = [table_ref[map_ref[dev, list_ref[leaf, col + s]]] for s in range(4)]
            both = jnp.concatenate(
                [jnp.where(low, part[0], part[1]), jnp.where(low, part[2], part[3])], axis=1
            )
            squared = dot(target_ref[leaf], both[16:])
            weights = lax.rsqrt(squared).astype(BF16)
            sum_ref[leaf] += dot(both[:16], weights, NT)
        return carry

    lax.fori_loop(0, (item_ref[8, 0] + (UNEAR - 1)) // UNEAR, step, 0)
    for t in range(64):
        out_ref[:, 128 * t : 128 * t + 128] = jnp.concatenate(
            [sum_ref[2 * t], sum_ref[2 * t + 1]], axis=1
        )


def top_kernel(n_sub, dev_ref, transfer_ref, *refs):
    root_refs, out_ref = refs[:n_sub], refs[n_sub]
    sub = lax.rem(dev_ref[0], n_sub)
    coef = jnp.zeros((16, 128), F32)
    centre = jnp.zeros((8, 128), F32)
    for k in range(n_sub):
        owner = lax.rem(sub + n_sub - k, n_sub)
        for b in range(2):
            c = lax.rem(owner * 2 + b, 8)
            e = transfer_ref[pl.ds(pl.multiple_of(c * 32, 32), 32), :]
            e4 = jnp.concatenate([e] * 4, axis=1)
            coef = coef + dot(root_refs[k][16 * b : 16 * b + 16, 0:32], e4, precision=HI)
            centre = centre + root_refs[k][32 + 8 * b : 40 + 8 * b, :]
    out_ref[0:16, :] = coef
    out_ref[16:24, :] = centre * (1.0 / (2 * n_sub))


def far_kernel(
    n_sub,
    n_leaf,
    dev_ref,
    item_ref,
    list_ref,
    mid_list_ref,
    root_list_ref,
    top_list_ref,
    near_ref,
    basis_ref,
    transfer_ref,
    proxy_ref,
    coef_ref,
    mid_ref,
    centre_ref,
    prev_ref,
    next_ref,
    *refs,
):
    root_refs = refs[:n_sub]
    top_refs = refs[n_sub : n_sub + n_leaf]
    out_ref, table_ref, target_ref, sum_ref, mtable_ref, mtarget_ref, mout_ref, small_ref = refs[
        n_sub + n_leaf :
    ]
    dev = dev_ref[0]
    sub = lax.rem(dev, n_sub)
    top = lax.div(dev, n_sub)
    origin = origin8(dev * 128)
    identity = eye(128)
    proxy8 = rows8(jnp.concatenate([proxy_ref[...]] * 4, axis=1))
    group64 = iota((64, 128), 1) // 32
    group48 = iota((48, 128), 1) // 32
    f3 = iota((8, 128), 0) % 4 == 3

    def shifted(c8, radius):
        return jnp.where(f3, 0.0, (c8 - origin + radius * proxy8) * SCALE)

    mean8 = jnp.where(iota((128, 128), 0) // 8 == iota((128, 128), 1), 0.125, 0.0)
    own_c8 = None
    for way, block in enumerate((prev_ref, None, next_ref)):
        packed = centre_ref[...] if way == 1 else block[ROW_K : ROW_K + 16, :]
        c8 = unpack16(packed)
        spread = expand_centres(c8, 32)
        for t in range(32):
            u8 = shifted(spread[8 * t : 8 * t + 8], 1.0)
            at = slice(16 * t, 16 * t + 16)
            coef = coef_ref[at, :] if way == 1 else block[ROW_C + 16 * t : ROW_C + 16 * t + 16, :]
            tiles = four_tiled(
                jnp.concatenate([coef.astype(F32), source_rows(u8)], axis=0), group48
            )
            for h in range(4):
                table_ref[128 * way + 4 * t + h] = tiles[h].astype(BF16)
            if way == 1:
                turn = turned(target_rows(u8), identity)
                for h in range(4):
                    target_ref[4 * t + h] = turn[32 * h : 32 * h + 32]
        m8 = dot(c8, mean8, precision=HI)
        spread = expand_centres(m8, 4)
        for t in range(4):
            u8 = shifted(spread[8 * t : 8 * t + 8], 2.0)
            if way == 1:
                high = mid_ref[16 * t : 16 * t + 16, :]
                rest = mid_ref[64 + 16 * t : 64 + 16 * t + 16, :]
            else:
                high = block[ROW_MH + 16 * t : ROW_MH + 16 * t + 16, :]
                rest = block[ROW_ML + 16 * t : ROW_ML + 16 * t + 16, :]
            tiles = four_tiled(
                jnp.concatenate([high.astype(F32), rest.astype(F32), source_rows(u8)], axis=0),
                group64,
            )
            for h in range(4):
                mtable_ref[16 * way + 4 * t + h] = tiles[h].astype(BF16)
            if way == 1:
                turn = turned(target_rows(u8), identity)
                for h in range(4):
                    mtarget_ref[4 * t + h] = turn[32 * h : 32 * h + 32]
    table_ref[384] = jnp.where(iota((48, 128), 0) < 16, 0.0, table_ref[128].astype(F32)).astype(BF16)
    mtable_ref[48] = jnp.where(iota((64, 128), 0) < 32, 0.0, mtable_ref[16].astype(F32)).astype(BF16)
    target_ref[128] = target_ref[0]
    sum_ref[...] = jnp.zeros_like(sum_ref)

    def step(it, carry):
        for u in range(UFAR):
            k = it * UFAR + u
            packed = item_ref[k >> 7, k & 127]
            leaf = packed >> 4
            col = (packed & 15) * 8
            part = [table_ref[list_ref[leaf, col + s]] for s in range(8)]
            both = jnp.concatenate(
                [
                    jnp.where(
                        group48 < 2,
                        jnp.where(group48 == 0, part[h], part[h + 1]),
                        jnp.where(group48 == 2, part[h + 2], part[h + 3]),
                    )
                    for h in (0, 4)
                ],
                axis=1,
            )
            squared = dot(target_ref[leaf], both[16:])
            weights = lax.rsqrt(squared).astype(BF16)
            sum_ref[leaf] += dot(both[:16], weights, NT)
        return carry

    lax.fori_loop(0, (item_ref[8, 0] + (UFAR - 1)) // UFAR, step, 0)

    def couple(target, rows, table):
        while len(rows) % 4:
            rows.append(jnp.int32(-1))
        tiles = []
        for h in range(0, len(rows), 4):
            part = [table(r) for r in rows[h : h + 4]]
            tiles.append(
                jnp.where(
                    group64 < 2,
                    jnp.where(group64 == 0, part[0], part[1]),
                    jnp.where(group64 == 2, part[2], part[3]),
                )
            )
        both = jnp.concatenate(tiles, axis=1) if len(tiles) > 1 else tiles[0]
        weights = lax.rsqrt(dot(target, both[32:]))
        high = weights.astype(BF16)
        rest = (weights - high.astype(F32)).astype(BF16)
        first = dot(both[:32], high, NT)
        return first[:16] + first[16:] + dot(both[:16], rest, NT)

    def fill(slot, coef, u8):
        high = rounded(coef)
        small_ref[slot] = jnp.concatenate([high, coef - high, source_rows(u8)], axis=0).astype(BF16)

    empty_top, first_root = n_leaf, n_leaf + 1
    empty_root = first_root + 2 * n_sub
    blank = jnp.zeros((16, 128), F32)
    for k in range(n_leaf):
        fill(k, top_refs[k][0:16, :], shifted(top_refs[k][16:24, :], 8.0))
    fill(empty_top, blank, shifted(top_refs[0][16:24, :], 8.0))
    for k in range(n_sub):
        for b in range(2):
            fill(
                first_root + 2 * k + b,
                root_refs[k][16 * b : 16 * b + 16, :],
                shifted(root_refs[k][32 + 8 * b : 40 + 8 * b, :], 4.0),
            )
    fill(empty_root, blank, shifted(root_refs[0][32:40, :], 4.0))

    rows = []
    for s in range(top_list_ref.shape[1]):
        j = top_list_ref[top, s]
        rows.append(jnp.where(j >= 0, lax.rem(top - j + n_leaf, n_leaf), -1))
    target = turned(target_rows(shifted(top_refs[0][16:24, :], 8.0)), identity)[:32]
    top_out = couple(target, rows, lambda r: small_ref[jnp.where(r >= 0, r, empty_top)])
    root_out = []
    for b in range(2):
        rows = []
        for s in range(root_list_ref.shape[1]):
            j = root_list_ref[b, s]
            inside = j - top * (2 * n_sub)
            shift = lax.rem(sub - (inside >> 1) + n_sub, n_sub)
            rows.append(jnp.where(j >= 0, 2 * shift + (inside & 1), -1))
        target = turned(
            target_rows(shifted(root_refs[0][32 + 8 * b : 40 + 8 * b, :], 4.0)), identity
        )[:32]
        far_in = couple(
            target, rows, lambda r: small_ref[jnp.where(r >= 0, first_root + r, empty_root)]
        )
        c = lax.rem(sub * 2 + b, 8)
        e = transfer_ref[pl.ds(pl.multiple_of(c * 32, 32), 32), :]
        root_out.append(far_in + dot(top_out, e, NT, HI))
    for b in range(2):
        down = dot(root_out[b], transfer_ref[...], NT, HI)
        for c in range(8):
            m = 8 * b + c
            rows = []
            for s in range(mid_list_ref.shape[1]):
                j = mid_list_ref[m, s]
                rows.append(jnp.where(j >= 0, j - dev * 16 + 16, -1))
            far_in = couple(
                mtarget_ref[m], rows, lambda r: mtable_ref[jnp.where(r >= 0, r, 48)]
            )
            mout_ref[16 * m : 16 * m + 16, :] = far_in + down[:, 32 * c : 32 * c + 32]
    down = dot(mout_ref[...], transfer_ref[...], NT, HI)
    for m in range(16):
        for half in range(2):
            t = 2 * m + half
            far_in = jnp.concatenate([sum_ref[4 * t + h] for h in range(4)], axis=1)
            leaf_out = far_in + down[16 * m : 16 * m + 16, 128 * half : 128 * half + 128]
            cols = slice(256 * t, 256 * t + 256)
            out_ref[:, cols] = near_ref[:, cols] + dot(
                leaf_out.astype(BF16), diagonal_basis(basis_ref[:, cols])
            )


def cells_of(index):
    out = np.zeros(index.shape + (3,), np.int64)
    for axis in range(3):
        for bit in range(8):
            out[..., axis] |= ((index >> (3 * bit + axis)) & 1) << bit
    return out


@functools.cache
def near_plan(devices, leaves):
    pairs = np.zeros((devices, 2 * PAIRS), np.int32)
    for dev in range(devices):
        own = cells_of(np.arange(leaves) + dev * leaves)
        for way, other in ((0, dev + 1), (1, dev - 1)):
            if not 0 <= other < devices:
                continue
            theirs = cells_of(np.arange(leaves) + other * leaves)
            low, high = theirs.min(0) - 1, theirs.max(0) + 1
            touch = ((own >= low) & (own <= high)).all(1)
            found = np.unique(np.nonzero(touch)[0] // 2)
            assert len(found) <= PAIRS
            pairs[dev, way * PAIRS : way * PAIRS + len(found)] = found
    rows = np.full((devices, 3 * leaves + 1), 192, np.int32)
    for dev in range(devices):
        rows[dev, leaves : 2 * leaves] = np.arange(leaves)
        for way, other, first in ((0, dev - 1, 0), (1, dev + 1, 2 * leaves)):
            if not 0 <= other < devices:
                continue
            for k in reversed(range(PAIRS)):
                pair = pairs[other, way * PAIRS + k]
                for odd in range(2):
                    rows[dev, first + 2 * pair + odd] = 128 + 2 * (PAIRS * way + k) + odd
    return pairs, rows


def around(x, axis, count):
    out = [x]
    for k in range(1, count):
        out.append(lax.ppermute(x, axis, [(i, (i + k) % count) for i in range(count)]))
    return out


SMEM = pl.BlockSpec(memory_space=pltpu.SMEM)
VMEM = pl.BlockSpec(memory_space=pltpu.VMEM)


def call(kernel, name, in_specs, outs, scratch, cost):
    return pl.pallas_call(
        kernel,
        name=name,
        in_specs=in_specs,
        out_shape=outs,
        out_specs=jax.tree.map(lambda _: VMEM, outs),
        scratch_shapes=scratch,
        compiler_params=pltpu.CompilerParams(vmem_limit_bytes=48 << 20),
        cost_estimate=pl.CostEstimate(flops=cost, bytes_accessed=1 << 20, transcendentals=0),
    )


def body(
    vectors,
    points,
    leaf_basis,
    transfer,
    proxy_points,
    near_list,
    far_leaf,
    far_mid,
    far_root,
    far_top,
):
    shape = jax.ShapeDtypeStruct
    n_sub, n_leaf = lax.axis_size("sub"), lax.axis_size("leaf")
    devices = n_sub * n_leaf
    along = ("leaf", "sub")
    device = lax.axis_index(along).astype(jnp.int32).reshape(1)
    pairs, near_rows = near_plan(devices, near_list.shape[0])
    matrices = transfer.reshape(256, 32)
    ahead, back, roots, coef, mid, centre, near_items, far_items, near_local, far_local = call(
        local_kernel,
        "local",
        [SMEM, SMEM] + [VMEM] * 6,
        (
            shape((ROWS, 128), BF16),
            shape((ROWS, 128), BF16),
            shape((48, 128), F32),
            shape((512, 128), BF16),
            shape((128, 128), BF16),
            shape((16, 128), BF16),
            shape((16, 128), jnp.int32),
            shape((16, 128), jnp.int32),
            shape((136, 28), jnp.int32),
            shape((136, 64), jnp.int32),
        ),
        [pltpu.VMEM((8, 8192), F32)],
        1 << 30,
    )(device, jnp.asarray(pairs), vectors, points, leaf_basis, matrices, near_list, far_leaf)
    from_prev = lax.ppermute(ahead, along, [(i, i + 1) for i in range(devices - 1)])
    from_next = lax.ppermute(back, along, [(i + 1, i) for i in range(devices - 1)])
    row_roots = around(roots, "sub", n_sub)
    top = call(
        functools.partial(top_kernel, n_sub),
        "top",
        [SMEM] + [VMEM] * (1 + n_sub),
        shape((24, 128), F32),
        [],
        1 << 20,
    )(device, matrices, *row_roots)
    tops = around(top, "leaf", n_leaf)
    near = call(
        near_kernel,
        "near",
        [SMEM] * 4 + [VMEM] * 4,
        shape((16, 8192), F32),
        [
            pltpu.VMEM((193, 48, 128), BF16),
            pltpu.VMEM((129, 64, 32), BF16),
            pltpu.VMEM((129, 16, 64), F32),
        ],
        1 << 33,
    )(device, near_items, near_local, jnp.asarray(near_rows), vectors, points, from_prev, from_next)
    return call(
        functools.partial(far_kernel, n_sub, n_leaf),
        "far",
        [SMEM] * 6 + [VMEM] * (9 + n_sub + n_leaf),
        shape((16, 8192), F32),
        [
            pltpu.VMEM((385, 48, 128), BF16),
            pltpu.VMEM((129, 32, 32), BF16),
            pltpu.VMEM((129, 16, 32), F32),
            pltpu.VMEM((49, 64, 128), BF16),
            pltpu.VMEM((16, 32, 32), BF16),
            pltpu.VMEM((256, 32), F32),
            pltpu.VMEM((n_leaf + 2 + 2 * n_sub, 64, 128), BF16),
        ],
        1 << 33,
    )(
        device,
        far_items,
        far_local,
        far_mid,
        far_root,
        far_top,
        near,
        leaf_basis,
        matrices,
        proxy_points,
        coef,
        mid,
        centre,
        from_prev,
        from_next,
        *row_roots,
        *tops,
    )


def solution(mesh):
    return jax.shard_map(
        body,
        mesh=mesh,
        in_specs=(
            P("vec", ("groups", "leaf", "sub")),
            P(None, ("groups", "leaf", "sub")),
            P(None, ("groups", "leaf", "sub")),
            P(),
            P(),
            P(("groups", "leaf", "sub"), None),
            P(("groups", "leaf", "sub"), None),
            P(("groups", "leaf", "sub"), None),
            P(("groups", "leaf", "sub"), None),
            P("groups", None),
        ),
        out_specs=P("vec", ("groups", "leaf", "sub")),
        check_vma=False,
    )
```
